32 devices in a mesh: groups: 2 (over x), tp: 16 (over z, y, core).
Axes of the slice: x: 2, y: 2, z: 4, core: 2. Of those that a mesh axis runs over, the one named last changes fastest.
Arguments:
- residual: bfloat16 [2, 8, 16384], P(None, 'groups', 'tp'), parts along dimension 1, may hold values from -4 to 4, as said below
- norm_gain: bfloat16 [16384], P('tp'), may hold values from 0.099609375 to 1.8984375
- w_query: bfloat16 [16384, 8192], P('tp'), may hold values from -0.046875 to 0.046875
- w_keyval: bfloat16 [16384, 2048], P('tp'), may hold values from -0.046875 to 0.046875
- w_out: bfloat16 [8192, 16384], P('tp'), may hold values from -0.75 to 0.75
- kv_cache: bfloat16 [8, 4096, 2048], P('groups', 'tp'), parts along dimension 0, may hold values from -103 to 103
- lengths: int32 [8], P('groups'), parts along dimension 0, may hold values from 1 to 4096, 8192 in all
Outputs:
- hidden_out: bfloat16 [2, 8, 16384], P(None, 'groups', 'tp'), parts along dimension 1
The draws below stay inside these ranges and needn't reach their ends.
There are 2 independent parts, one for each index of `groups`. The reference program is written for one: setup_inputs(seed, part) draws one part's arguments, and reference() takes and returns one part's arrays. A program takes and returns all parts, laid end to end along the dimension named above; an argument that names none is the same for every part. Nothing has to cross between parts.
Inputs may be any that keep to these rules, and one draw needn't show every extreme that they name: `residual`: the layer's input rows. `lengths`: some row fills all 4096 cache positions.
All inputs are finite; a program needn't handle non-finite values.
Results may differ from the reference program's by a relative error of at most 0.015.
The reference program's roundings to bfloat16 on the way (of `normed`, `new_values` and `attended`) count: a program that leaves them out, or rounds other values in their place, can miss the bound.
Values may be sent and summed in bfloat16 or wider, within the bound.
A program may use at most 128 MiB of HBM per device.

```python
import math
import jax
import jax.numpy as jnp
import numpy as np
from jax import lax

D = 16384
QH = 64
KVH = 8
HD = 128
STEPS = 2
ROWS = 4
CL = 256
CACHE_LEN = 4096
N_TP = 16


def draw_residual(key, part):
    key = jax.random.fold_in(key, 7)
    noise_key = jax.random.fold_in(key, 0)
    full_shape = (STEPS, ROWS, D)
    column = jnp.arange(D, dtype=jnp.float32) / D
    values = jnp.clip(jax.random.normal(noise_key, full_shape, jnp.float32), -4.0, 4.0) * 3.0 ** column / 10.0
    return values.astype(jnp.bfloat16)


def draw_kv_cache(key, part):
    key = jax.random.fold_in(key, 23)
    noise_key = jax.random.fold_in(key, 0)
    full_shape = (ROWS, CACHE_LEN, 2 * KVH * HD)
    values = jnp.clip(jax.random.normal(noise_key, full_shape, jnp.float32), -4.0, 4.0)
    return values.astype(jnp.bfloat16)


def spiked(array, rng, source, target, parts, factor):
    def block_of(axis_at):
        return (jnp.arange(array.shape[axis_at]) // (array.shape[axis_at] // parts)).reshape((-1,) + (1,) * (array.ndim - 1 - axis_at))

    first = jax.random.permutation(rng, parts)[block_of(target)]
    other_side = (block_of(target) + parts // 2) % parts
    return jnp.where((block_of(source) == first) | (block_of(source) == other_side), factor * array, array)


def shard_levels(key, extent, pieces, least, top_value):
    factor_of = 1.0
    for dim, parts in pieces:
        steps = jax.random.uniform(jax.random.fold_in(jax.random.fold_in(key, 6), dim), (parts,), jnp.float32, least / len(pieces), top_value / len(pieces))
        factor_of = factor_of * jnp.repeat(jnp.exp(steps), extent[dim] // parts).reshape((-1,) + (1,) * (len(extent) - 1 - dim))
    return factor_of


def length_profile(number_of, total, bound, slope):
    weights = [(1 << 20) // math.isqrt(grade ** slope) + 1 for grade in range(2, number_of + 1)]
    rest, given = total - bound - (number_of - 1), [1] * (number_of - 1)
    while rest > 0:
        movable = [i for i in range(number_of - 1) if given[i] < bound]
        mass, left = sum([weights[i] for i in movable]), rest
        for i in movable:
            extra = min(bound - given[i], max(1, left * weights[i] // mass), rest)
            given[i] = given[i] + extra
            rest = rest - extra
    return np.array([bound] + given)


def uneven_parts(rng, number_of, total, most, skew):
    if number_of == 2:
        one = jax.random.randint(rng, (), max(1, total - most), min(most, total - 1) + 1)
        return jnp.stack([one, total - one])
    tallies = jnp.asarray(length_profile(number_of, total, most, skew), jnp.int32)
    twos = (number_of - 1) // 2
    giver, receiver = tallies[1:1 + 2 * twos:2], tallies[2:2 + 2 * twos:2]
    slack = jnp.minimum(giver - 1, most - receiver)
    passed = jax.random.randint(jax.random.fold_in(rng, 1), (twos,), 0, 1 << 20) % (slack + 1)
    tallies = tallies.at[1:1 + 2 * twos:2].set(giver - passed).at[2:2 + 2 * twos:2].set(receiver + passed)
    return tallies[jax.random.permutation(jax.random.fold_in(rng, 2), number_of)]


def scatter_about(key, shape, width, limit, cuts=(), kind=jnp.bfloat16):
    gain = shard_levels(key, shape, cuts, -0.22, 0.18) if cuts else 1.0
    values = jax.random.normal(key, shape, jnp.float32) * width * gain
    return jnp.minimum(jnp.maximum(values, -limit), limit).astype(kind)


def gaussian_with(own_key, dims, spread, limit, cuts, heavy, kind=jnp.bfloat16):
    result = spread * jax.random.normal(own_key, dims, jnp.float32)
    if cuts:
        result = result * shard_levels(own_key, dims, cuts, -0.22, 0.18)
    return jnp.clip(spiked(result, jax.random.fold_in(own_key, 3), *heavy), -limit, limit).astype(kind)


def setup_inputs(seed: int = 0, part: int = 0) -> dict:
    splits = jax.random.split(jax.random.key(seed), 8)
    own_keys = jax.random.split(jax.random.fold_in(splits[7], part), 8)
    residual = draw_residual(jax.random.fold_in(jax.random.fold_in(splits[7], part), 71), part)
    norm_gain = jnp.clip(1.0 + 0.18 * jax.random.normal(splits[1], (D,), jnp.float32), 0.099609375, 1.8984375).astype(jnp.bfloat16)
    w_query = scatter_about(splits[2], (D, QH * HD), D ** -0.5, 0.046875, ((0, 16),))
    w_keyval = scatter_about(splits[3], (D, 2 * KVH * HD), D ** -0.5, 0.046875, ((0, 16),))
    w_out = gaussian_with(splits[4], (QH * HD, D), HD ** -0.5, 0.75, ((0, 16),), (0, 1, 16, 2.0))
    kv_cache = draw_kv_cache(jax.random.fold_in(jax.random.fold_in(splits[7], part), 71), part)
    lengths = uneven_parts(own_keys[6], ROWS, ROWS * CACHE_LEN // 2, CACHE_LEN, 2).astype(jnp.int32)
    return {"residual": residual, "norm_gain": norm_gain, "w_query": w_query, "w_keyval": w_keyval, "w_out": w_out, "kv_cache": kv_cache, "lengths": lengths}


def rotate(vectors, position):
    halfway = vectors.shape[-1] // 2
    frequency = 500000.0 ** (-2.0 * jnp.arange(halfway, dtype=jnp.float32) / vectors.shape[-1])
    angles = position[..., None, None].astype(jnp.float32) * frequency
    cosine = jnp.cos(angles)
    sine_part = jnp.sin(angles)
    leading = vectors[..., :halfway]
    trailing = vectors[..., halfway:]
    return jnp.concatenate([leading * cosine - trailing * sine_part, trailing * cosine + leading * sine_part], axis=-1)

def reference(residual, norm_gain, w_query, w_keyval, w_out, kv_cache, lengths):
    inv_root = HD ** (-0.5)
    group_size = QH // KVH
    wide_residual = residual.astype(jnp.float32)
    squares = lax.optimization_barrier(jnp.sum(wide_residual * wide_residual, axis=-1))
    scaling = lax.rsqrt(squares / D + 1e-05)
    normed = (wide_residual * scaling[..., None] * norm_gain.astype(jnp.float32)).astype(jnp.bfloat16)
    flat_rows = normed.reshape(STEPS * ROWS, D)
    query_total = jnp.dot(flat_rows, w_query, preferred_element_type=jnp.float32)
    keyval_total = jnp.dot(flat_rows, w_keyval, preferred_element_type=jnp.float32)
    position = lengths[None, :] + jnp.arange(STEPS, dtype=jnp.int32)[:, None]
    queries = rotate(query_total.reshape(STEPS, ROWS, QH, HD), position).astype(jnp.bfloat16)
    queries = queries.reshape(STEPS, ROWS, KVH, group_size, HD).astype(jnp.float32)
    keyval_total = keyval_total.reshape(STEPS, ROWS, 2, KVH, HD)
    new_keys = rotate(keyval_total[:, :, 0], position).astype(jnp.bfloat16).astype(jnp.float32)
    new_values = keyval_total[:, :, 1].astype(jnp.bfloat16).astype(jnp.float32)
    cache_keys = kv_cache[:, :, :KVH * HD].reshape(ROWS, CACHE_LEN, KVH, HD).astype(jnp.float32)
    cache_values = kv_cache[:, :, KVH * HD:].reshape(ROWS, N_TP, CL, KVH, HD).astype(jnp.float32)
    valid = jnp.arange(CACHE_LEN, dtype=jnp.int32)[None, :] < lengths[:, None]
    live_slots = valid.reshape(ROWS, N_TP, CL)[None, :, None, None, :, :]
    cached = jnp.einsum('srkgd,rlkd->srkgl', queries, cache_keys) * inv_root
    blocked = cached.reshape(STEPS, ROWS, KVH, group_size, N_TP, CL)
    masked = jnp.where(live_slots, blocked, -1e+30)
    block_top = lax.optimization_barrier(jnp.max(masked, axis=-1))
    fresh = jnp.einsum('srkgd,urkd->srkgu', queries, new_keys) * inv_root
    causal = jnp.arange(STEPS)[:, None] >= jnp.arange(STEPS)[None, :]
    fresh = jnp.where(causal[:, None, None, None, :], fresh, -1e+30)
    top = jnp.maximum(lax.optimization_barrier(jnp.max(block_top, axis=-1)), lax.optimization_barrier(jnp.max(fresh, axis=-1)))
    block_weights = jnp.where(live_slots, jnp.exp(masked - block_top[..., None]), 0.0)
    block_weights = block_weights.astype(jnp.bfloat16).astype(jnp.float32)
    fresh_weights = jnp.exp(fresh - top[..., None]).astype(jnp.bfloat16).astype(jnp.float32)
    rescale = jnp.exp(block_top - top[..., None])
    totals = lax.optimization_barrier(jnp.sum(rescale * lax.optimization_barrier(jnp.sum(block_weights, axis=-1)), axis=-1)) + lax.optimization_barrier(jnp.sum(fresh_weights, axis=-1))
    block_values = jnp.einsum('srkgbl,rblkd->srkgbd', block_weights, cache_values)
    summed_values = lax.optimization_barrier(jnp.sum(block_values * rescale[..., None], axis=4))
    summed_values = summed_values + jnp.einsum('srkgu,urkd->srkgd', fresh_weights, new_values)
    attended = (summed_values / totals[..., None]).astype(jnp.bfloat16)
    attended = attended.reshape(STEPS * ROWS, N_TP, QH * HD // N_TP).transpose(1, 0, 2)
    blocks = w_out.reshape(N_TP, QH * HD // N_TP, D)

    def add_block(running, operands):
        partial_value = jnp.dot(operands[0], operands[1], preferred_element_type=jnp.float32).astype(jnp.bfloat16)
        return (running + partial_value.astype(jnp.float32), None)
    summed, ignored = lax.scan(add_block, jnp.zeros((STEPS * ROWS, D), jnp.float32), (attended, blocks))
    return (wide_residual + summed.reshape(STEPS, ROWS, D)).astype(jnp.bfloat16)
```

```python
import functools

import jax
import jax.numpy as jnp
from jax import lax
from jax.experimental import pallas as pl
from jax.experimental.pallas import tpu as pltpu
from jax.sharding import PartitionSpec as P

QH = 64
KVH = 8
HD = 128
UNITS = 2 * KVH
GROUP = QH // KVH
LIVE_MIN = -1e30
MESH = pl.DeviceIdType.MESH
SQ, QKV, GATHER, MERGE, PROJ = range(5)


def kernel(
    n,
    len_ref, res_ref, gain_ref, cos_ref, sin_ref, wq_hbm, wkv_hbm, wo_hbm, kv_hbm,
    out_ref,
    wq_v, wkv_v, wo_v, kv_v, sq_buf, kv_part, q_send, q_recv, gathered,
    o_send, o_recv, p_send, p_recv,
    wq_sem, wkv_sem, wo_sem, kv_sem, send_sem, recv_sem,
):
    steps, requests, width = res_ref.shape
    rows = steps * requests
    window = kv_hbm.shape[1]
    features = width * n
    heads = QH // n
    columns = heads * HD
    head_rows = heads * rows
    per_kv = n // KVH
    per_unit = n // UNITS
    me = lax.axis_index("tp")

    def peer_at(i):
        return lax.rem(me + i, n)

    def source_at(i):
        return lax.rem(me - i + n, n)

    def remote(phase, i, src, dst, peer):
        return pltpu.make_async_remote_copy(
            src_ref=src,
            dst_ref=dst,
            send_sem=send_sem.at[phase, i],
            recv_sem=recv_sem.at[phase, i],
            device_id={"tp": peer},
            device_id_type=MESH,
        )

    def each_peer(body):
        lax.fori_loop(1, n, lambda i, c: (body(i), c)[1], 0)

    def wq_copy(i):
        at = pl.multiple_of(peer_at(i) * columns, columns)
        return pltpu.make_async_copy(wq_hbm.at[:, pl.ds(at, columns)], wq_v.at[i], wq_sem.at[i])

    def wo_copy(i):
        at = pl.multiple_of(peer_at(i) * width, width)
        return pltpu.make_async_copy(wo_hbm.at[:, pl.ds(at, width)], wo_v.at[i], wo_sem.at[i])

    wkv_copy = pltpu.make_async_copy(wkv_hbm, wkv_v, wkv_sem)
    kv_copy = pltpu.make_async_copy(kv_hbm, kv_v, kv_sem)
    wkv_copy.start()
    each_peer(lambda i: wq_copy(i).start())
    wq_copy(0).start()

    barrier = pltpu.get_barrier_semaphore()
    each_peer(
        lambda i: pl.semaphore_signal(
            barrier, inc=1, device_id={"tp": peer_at(i)}, device_id_type=MESH
        )
    )
    residual = jnp.concatenate(
        [res_ref[s].astype(jnp.float32) for s in range(steps)], axis=0
    )
    sq_buf[me] = jnp.broadcast_to(
        jnp.sum(residual * residual, axis=-1, keepdims=True), (rows, HD)
    )
    pl.semaphore_wait(barrier, n - 1)

    each_peer(lambda i: remote(SQ, i, sq_buf.at[me], sq_buf.at[me], peer_at(i)).start())
    each_peer(
        lambda i: remote(SQ, i, sq_buf.at[me], sq_buf.at[source_at(i)], peer_at(i)).wait_recv()
    )
    squares = jnp.sum(sq_buf[...], axis=0)[:, :1]
    scaling = lax.rsqrt(squares / features + 1e-05)
    normed = (residual * scaling * gain_ref[...].astype(jnp.float32)).astype(jnp.bfloat16)

    wkv_copy.wait()

    def keyval(c, carry):
        at = pl.multiple_of(c * 512, 512)
        kv_part[:, pl.ds(at, 512)] = jnp.dot(
            normed, wkv_v[:, pl.ds(at, 512)], preferred_element_type=jnp.float32
        )
        return carry

    lax.fori_loop(0, kv_part.shape[1] // 512, keyval, 0)

    def project(i, target):
        wq_copy(i).wait()
        wo_copy(i).start()
        at = pl.multiple_of(peer_at(i) // per_unit * HD, HD)
        target[:, :columns] = jnp.dot(normed, wq_v[i], preferred_element_type=jnp.float32)
        target[:, columns:] = kv_part[:, pl.ds(at, HD)]

    def project_send(i):
        project(i, q_send.at[i])
        remote(QKV, i, q_send.at[i], q_recv.at[me], peer_at(i)).start()

    each_peer(project_send)
    kv_copy.start()
    project(0, q_recv.at[me])
    each_peer(
        lambda i: remote(QKV, i, q_send.at[i], q_recv.at[source_at(i)], peer_at(i)).wait_recv()
    )

    total = jnp.sum(q_recv[...], axis=0)
    cosine = cos_ref[...]
    sine = sin_ref[...]

    def rotated(v):
        return v * cosine + pltpu.roll(v, HD // 2, 1) * sine

    units = [rotated(total[:, u * HD : (u + 1) * HD]) for u in range(heads)]
    last = total[:, columns:]
    units.append(jnp.where(me // per_unit < KVH, rotated(last), last))
    while len(units) * rows < gathered.shape[1]:
        units.append(jnp.zeros((rows, HD), jnp.float32))
    gathered[me] = jnp.concatenate(units, axis=0).astype(jnp.bfloat16)
    each_peer(
        lambda i: remote(GATHER, i, gathered.at[me], gathered.at[me], peer_at(i)).start()
    )
    kv_copy.wait()
    each_peer(
        lambda i: remote(
            GATHER, i, gathered.at[me], gathered.at[source_at(i)], peer_at(i)
        ).wait_recv()
    )

    inv_root = HD ** (-0.5)
    q_rows = GROUP * rows
    request_of = lax.broadcasted_iota(jnp.int32, (q_rows, window), 0) % requests
    slot = me * window + lax.broadcasted_iota(jnp.int32, (q_rows, window), 1)
    length_of = jnp.full((q_rows, window), len_ref[0], jnp.int32)
    for r in range(1, requests):
        length_of = jnp.where(request_of == r, len_ref[r], length_of)
    live = slot < length_of
    lane = lax.broadcasted_iota(jnp.int32, (rows, HD), 1)

    def attend(step, carry):
        k = lax.rem(me // per_kv + 1 + step, KVH)
        key_at = pl.multiple_of(k * HD, HD)
        value_at = pl.multiple_of((KVH + k) * HD, HD)
        queries = jnp.concatenate(
            [gathered[k * per_kv + j, :head_rows, :] for j in range(per_kv)], axis=0
        )
        keys = kv_v[:, :, pl.ds(key_at, HD)].reshape(requests * window, HD)
        values = kv_v[:, :, pl.ds(value_at, HD)].reshape(requests * window, HD)
        scores = lax.dot_general(
            queries, keys, (((1,), (1,)), ((), ())), preferred_element_type=jnp.float32
        )
        cached = scores[:, :window]
        for r in range(1, requests):
            cached = jnp.where(
                request_of == r, scores[:, r * window : (r + 1) * window], cached
            )
        cached = jnp.where(live, cached * inv_root, LIVE_MIN)
        top = jnp.max(cached, axis=-1, keepdims=True)
        weights = jnp.where(live, jnp.exp(cached - top), 0.0)
        weights = weights.astype(jnp.bfloat16).astype(jnp.float32)
        weight_total = jnp.sum(weights, axis=-1, keepdims=True)
        spread = jnp.concatenate(
            [jnp.where(request_of == r, weights, 0.0) for r in range(requests)], axis=1
        ).astype(jnp.bfloat16)
        weighted = jnp.dot(spread, values, preferred_element_type=jnp.float32)
        for j in range(per_kv):
            d = k * per_kv + j
            first = j * head_rows
            stats = jnp.zeros((rows, HD), jnp.float32)
            for u in range(heads):
                at = first + u * rows
                stats = jnp.where(lane == u, top[at : at + rows], stats)
                stats = jnp.where(lane == HD // 2 + u, weight_total[at : at + rows], stats)
            block = jnp.concatenate([weighted[first : first + head_rows], stats], axis=0)

            @pl.when(d == me)
            def _():
                o_recv[me] = block

            @pl.when(d != me)
            def _():
                i = lax.rem(d - me + n, n)
                o_send[i] = block
                remote(MERGE, i, o_send.at[i], o_recv.at[me], d).start()

        return carry

    lax.fori_loop(0, KVH, attend, 0)

    my_kv = me // per_kv

    def unit_rows(u):
        return gathered[u * per_unit, head_rows : head_rows + 16, :].astype(jnp.float32)[:rows]

    new_keys = unit_rows(my_kv)
    new_values = unit_rows(KVH + my_kv)
    earlier_keys = pltpu.roll(new_keys, requests, 0)
    earlier_values = pltpu.roll(new_values, requests, 0)
    my_queries = gathered[me, :head_rows, :].astype(jnp.float32)
    second = lax.broadcasted_iota(jnp.int32, (rows, HD), 0) >= requests
    same = jnp.zeros((rows, HD), jnp.float32)
    earlier = jnp.zeros((rows, HD), jnp.float32)
    for u in range(heads):
        q = my_queries[u * rows : (u + 1) * rows]
        same = jnp.where(lane == u, jnp.sum(q * new_keys, axis=-1, keepdims=True), same)
        earlier = jnp.where(
            lane == u, jnp.sum(q * earlier_keys, axis=-1, keepdims=True), earlier
        )
    same = same * inv_root
    earlier = jnp.where(second, earlier * inv_root, LIVE_MIN)

    each_peer(
        lambda i: remote(MERGE, i, o_send.at[i], o_recv.at[source_at(i)], peer_at(i)).wait_recv()
    )
    stats = [o_recv[d, head_rows:, :] for d in range(n)]
    top = jnp.maximum(same, earlier)
    for d in range(n):
        top = jnp.maximum(top, stats[d])
    same_weight = jnp.exp(same - top).astype(jnp.bfloat16).astype(jnp.float32)
    earlier_weight = jnp.exp(earlier - top).astype(jnp.bfloat16).astype(jnp.float32)
    denominator = same_weight + earlier_weight
    numerators = [
        same_weight[:, u : u + 1] * new_values + earlier_weight[:, u : u + 1] * earlier_values
        for u in range(heads)
    ]
    for d in range(n):
        rescale = jnp.exp(stats[d] - top)
        denominator += rescale * pltpu.roll(stats[d], HD // 2, 1)
        for u in range(heads):
            numerators[u] += rescale[:, u : u + 1] * o_recv[d, u * rows : (u + 1) * rows, :]
    attended = jnp.concatenate(
        [numerators[u] / denominator[:, u : u + 1] for u in range(heads)], axis=1
    ).astype(jnp.bfloat16)

    half = width // 2

    def output(i, target):
        wo_copy(i).wait()
        y = jnp.dot(attended, wo_v[i], preferred_element_type=jnp.float32)
        target[...] = jnp.concatenate([y[:, :half], y[:, half:]], axis=0).astype(jnp.bfloat16)

    def output_send(i):
        output(i, p_send.at[i])
        remote(PROJ, i, p_send.at[i], p_recv.at[me], peer_at(i)).start()

    each_peer(output_send)
    output(0, p_recv.at[me])
    each_peer(
        lambda i: remote(PROJ, i, p_send.at[i], p_recv.at[source_at(i)], peer_at(i)).wait_recv()
    )
    summed = jnp.sum(p_recv[...].astype(jnp.float32), axis=0)
    summed = residual + jnp.concatenate([summed[:rows], summed[rows:]], axis=1)
    for s in range(steps):
        out_ref[s] = summed[s * requests : (s + 1) * requests].astype(jnp.bfloat16)

    def drain(i):
        remote(SQ, i, sq_buf.at[me], sq_buf.at[me], peer_at(i)).wait_send()
        remote(QKV, i, q_send.at[i], q_recv.at[me], peer_at(i)).wait_send()
        remote(GATHER, i, gathered.at[me], gathered.at[me], peer_at(i)).wait_send()
        remote(MERGE, i, o_send.at[i], o_recv.at[me], peer_at(i)).wait_send()
        remote(PROJ, i, p_send.at[i], p_recv.at[me], peer_at(i)).wait_send()

    each_peer(drain)


def on_device(n, residual, norm_gain, w_query, w_keyval, w_out, kv_cache, lengths):
    steps, requests, width = residual.shape
    rows = steps * requests
    heads = QH // n
    columns = heads * HD
    halfway = HD // 2
    position = lengths[None, :] + jnp.arange(steps, dtype=jnp.int32)[:, None]
    frequency = 500000.0 ** (-2.0 * jnp.arange(halfway, dtype=jnp.float32) / HD)
    angles = position.reshape(rows, 1).astype(jnp.float32) * frequency
    cosine = jnp.cos(angles)
    sine = jnp.sin(angles)
    cosine = jnp.concatenate([cosine, cosine], axis=-1)
    sine = jnp.concatenate([-sine, sine], axis=-1)

    gather_rows = ((heads + 1) * rows + 15) // 16 * 16
    vmem = pl.BlockSpec(memory_space=pltpu.VMEM)
    anywhere = pl.BlockSpec(memory_space=pl.ANY)
    bf16 = jnp.bfloat16
    f32 = jnp.float32
    return pl.pallas_call(
        functools.partial(kernel, n),
        out_shape=jax.ShapeDtypeStruct((steps, requests, width), bf16),
        in_specs=[pl.BlockSpec(memory_space=pltpu.SMEM), vmem, vmem, vmem, vmem]
        + [anywhere] * 4,
        out_specs=vmem,
        scratch_shapes=[
            pltpu.VMEM((n, width, columns), bf16),
            pltpu.VMEM(w_keyval.shape, bf16),
            pltpu.VMEM((n, w_out.shape[0], width), bf16),
            pltpu.VMEM(kv_cache.shape, bf16),
            pltpu.VMEM((n, rows, HD), f32),
            pltpu.VMEM((rows, w_keyval.shape[1]), f32),
            pltpu.VMEM((n, rows, columns + HD), f32),
            pltpu.VMEM((n, rows, columns + HD), f32),
            pltpu.VMEM((n, gather_rows, HD), bf16),
            pltpu.VMEM((n, (heads + 1) * rows, HD), f32),
            pltpu.VMEM((n, (heads + 1) * rows, HD), f32),
            pltpu.VMEM((n, 2 * rows, width // 2), bf16),
            pltpu.VMEM((n, 2 * rows, width // 2), bf16),
            pltpu.SemaphoreType.DMA((n,)),
            pltpu.SemaphoreType.DMA,
            pltpu.SemaphoreType.DMA((n,)),
            pltpu.SemaphoreType.DMA,
            pltpu.SemaphoreType.DMA((5, n)),
            pltpu.SemaphoreType.DMA((5, n)),
        ],
        compiler_params=pltpu.CompilerParams(
            collective_id=0, has_side_effects=True, vmem_limit_bytes=56 * 2**20
        ),
    )(lengths, residual, norm_gain.reshape(1, width), cosine, sine, w_query, w_keyval, w_out, kv_cache)


def solution(mesh):
    placed = (
        P(None, "groups", "tp"),
        P("tp"),
        P("tp", None),
        P("tp", None),
        P("tp", None),
        P("groups", "tp", None),
        P("groups"),
    )
    return jax.shard_map(
        functools.partial(on_device, mesh.shape["tp"]),
        mesh=mesh,
        in_specs=placed,
        out_specs=P(None, "groups", "tp"),
        check_vma=False,
    )
```

```python
import functools

import jax
import jax.numpy as jnp
from jax import lax
from jax.experimental import pallas as pl
from jax.experimental.pallas import tpu as pltpu
from jax.sharding import PartitionSpec as P

QH = 64
KVH = 8
HD = 128
UNITS = 2 * KVH
GROUP = QH // KVH
LIVE_MIN = -1e30
MESH = pl.DeviceIdType.MESH
SQ, QKV, GATHER, MERGE, PROJ = range(5)


def kernel(
    n,
    len_ref, res_ref, gain_ref, freq_ref, wq_hbm, wkv_hbm, wo_hbm, kv_hbm,
    out_ref,
    wq_v, wkv_v, wo_v, kv_v, sq_pair, sq_buf, kv_part,
    q_own, q_other, q_mate, q_recv, gathered,
    o_own, o_other, o_mate, o_recv, p_own, p_other, p_mate, p_recv,
    wq_sem, wkv_sem, wo_sem, kv_sem, send_sem, recv_sem,
):
    steps, requests, width = res_ref.shape
    rows = steps * requests
    window = kv_hbm.shape[1]
    features = width * n
    heads = QH // n
    columns = heads * HD
    head_rows = heads * rows
    per_kv = n // KVH
    per_unit = n // UNITS
    chips = n // 2
    me = lax.axis_index("tp")
    core = lax.rem(me, 2)
    chip = me // 2
    mate = me + 1 - 2 * core

    def chip_at(i):
        return lax.rem(chip + i, chips)

    def source_at(i):
        return lax.rem(chip - i + chips, chips)

    def peer_at(i):
        return chip_at(i) * 2 + core

    def across(phase, i, src, dst):
        return pltpu.make_async_remote_copy(
            src_ref=src,
            dst_ref=dst,
            send_sem=send_sem.at[phase, i],
            recv_sem=recv_sem.at[phase, i],
            device_id={"tp": peer_at(i)},
            device_id_type=MESH,
        )

    def to_mate(phase, i, src, dst):
        return pltpu.make_async_remote_copy(
            src_ref=src,
            dst_ref=dst,
            send_sem=send_sem.at[phase, chips + i],
            recv_sem=recv_sem.at[phase, chips + i],
            device_id={"tp": mate},
            device_id_type=MESH,
        )

    def each_peer(body):
        lax.fori_loop(1, chips, lambda i, c: (body(i), c)[1], 0)

    def each_chip(body):
        each_peer(body)
        body(0)

    def staggered(work, send):
        work(1)

        def both(i, carry):
            work(i)
            send(i - 1)
            return carry

        lax.fori_loop(2, chips, both, 0)
        work(0)
        send(chips - 1)

    def wq_copy(i):
        at = pl.multiple_of(chip_at(i) * (2 * columns), 2 * columns)
        return pltpu.make_async_copy(
            wq_hbm.at[:, pl.ds(at, 2 * columns)], wq_v.at[i], wq_sem.at[i]
        )

    def wo_copy(i):
        at = pl.multiple_of(chip_at(i) * (2 * width), 2 * width)
        return pltpu.make_async_copy(wo_hbm.at[:, pl.ds(at, 2 * width)], wo_v.at[i], wo_sem.at[i])

    wkv_copy = pltpu.make_async_copy(wkv_hbm, wkv_v, wkv_sem)
    kv_copy = pltpu.make_async_copy(kv_hbm, kv_v, kv_sem)

    barrier = pltpu.get_barrier_semaphore()
    pl.semaphore_signal(barrier, inc=1, device_id={"tp": mate}, device_id_type=MESH)
    each_peer(
        lambda i: pl.semaphore_signal(
            barrier, inc=1, device_id={"tp": peer_at(i)}, device_id_type=MESH
        )
    )
    wkv_copy.start()
    each_chip(lambda i: wq_copy(i).start())
    kv_copy.start()
    each_chip(lambda i: wo_copy(i).start())

    residual = jnp.concatenate(
        [res_ref[s].astype(jnp.float32) for s in range(steps)], axis=0
    )
    lane = lax.broadcasted_iota(jnp.int32, (rows, HD), 1)
    diagonal = lane == lax.broadcasted_iota(jnp.int32, (rows, HD), 0)
    own_squares = jnp.sum(residual * residual, axis=-1, keepdims=True)
    sq_pair[core] = jnp.sum(jnp.where(diagonal, own_squares, 0.0), axis=0, keepdims=True)
    row = lax.broadcasted_iota(jnp.int32, (rows, HD), 0)
    position = jnp.full((rows, HD), len_ref[0], jnp.int32)
    for r in range(1, requests):
        position = jnp.where(row % requests == r, len_ref[r], position)
    position = position + row // requests
    angles = position.astype(jnp.float32) * freq_ref[...]
    cosine = jnp.cos(angles)
    sine = jnp.sin(angles)
    sine = jnp.where(lane < HD // 2, -sine, sine)
    pl.semaphore_wait(barrier, chips)

    to_mate(SQ, 0, sq_pair.at[core], sq_pair.at[core]).start()
    to_mate(SQ, 0, sq_pair.at[core], sq_pair.at[1 - core]).wait_recv()
    sq_buf[chip] = sq_pair[0] + sq_pair[1]
    each_peer(lambda i: across(SQ, i, sq_buf.at[chip], sq_buf.at[chip]).start())
    each_peer(lambda i: across(SQ, i, sq_buf.at[chip], sq_buf.at[source_at(i)]).wait_recv())
    squares = jnp.sum(
        jnp.where(diagonal, jnp.sum(sq_buf[...], axis=0), 0.0), axis=-1, keepdims=True
    )
    scaling = lax.rsqrt(squares / features + 1e-05)
    normed = (residual * scaling * gain_ref[...].astype(jnp.float32).reshape(1, width)).astype(jnp.bfloat16)

    wkv_copy.wait()

    def keyval(c, carry):
        at = pl.multiple_of(c * 512, 512)
        kv_part[:, pl.ds(at, 512)] = jnp.dot(
            normed, wkv_v[:, pl.ds(at, 512)], preferred_element_type=jnp.float32
        )
        return carry

    lax.fori_loop(0, kv_part.shape[1] // 512, keyval, 0)

    def project(i):
        wq_copy(i).wait()
        y = jnp.dot(normed, wq_v[i], preferred_element_type=jnp.float32)
        first, second = y[:, :columns], y[:, columns:]
        for target, c in ((q_other, 1 - core), (q_own, core)):
            at = pl.multiple_of((chip_at(i) * 2 + c) // per_unit * HD, HD)
            target[i, :, :columns] = jnp.where(c == 0, first, second)
            target[i, :, columns:] = kv_part[:, pl.ds(at, HD)]
        to_mate(QKV, i, q_other.at[i], q_mate.at[i]).start()

    def project_send(i):
        to_mate(QKV, i, q_other.at[i], q_mate.at[i]).wait_recv()
        q_own[i] = q_own[i] + q_mate[i]
        across(QKV, i, q_own.at[i], q_recv.at[chip]).start()

    staggered(project, project_send)
    to_mate(QKV, 0, q_other.at[0], q_mate.at[0]).wait_recv()
    q_recv[chip] = q_own[0] + q_mate[0]
    each_peer(lambda i: across(QKV, i, q_own.at[i], q_recv.at[source_at(i)]).wait_recv())

    total = jnp.sum(q_recv[...], axis=0)

    def rotated(v):
        return v * cosine + pltpu.roll(v, HD // 2, 1) * sine

    units = [rotated(total[:, u * HD : (u + 1) * HD]) for u in range(heads)]
    last = total[:, columns:]
    units.append(jnp.where(me // per_unit < KVH, rotated(last), last))
    while len(units) * rows < gathered.shape[1]:
        units.append(jnp.zeros((rows, HD), jnp.float32))
    gathered[me] = jnp.concatenate(units, axis=0).astype(jnp.bfloat16)
    each_peer(lambda i: across(GATHER, i, gathered.at[me], gathered.at[me]).start())
    to_mate(GATHER, 0, gathered.at[me], gathered.at[me]).start()

    def forward(i):
        block = gathered.at[source_at(i) * 2 + core]
        across(GATHER, i, gathered.at[me], block).wait_recv()
        to_mate(GATHER, i, block, block).start()

    each_peer(forward)
    kv_copy.wait()

    def from_mate(i):
        block = gathered.at[source_at(i) * 2 + 1 - core]
        to_mate(GATHER, i, gathered.at[me], block).wait_recv()

    each_chip(from_mate)

    inv_root = HD ** (-0.5)
    q_rows = GROUP * rows
    request_of = lax.broadcasted_iota(jnp.int32, (q_rows, window), 0) % requests
    slot = me * window + lax.broadcasted_iota(jnp.int32, (q_rows, window), 1)
    length_of = jnp.full((q_rows, window), len_ref[0], jnp.int32)
    for r in range(1, requests):
        length_of = jnp.where(request_of == r, len_ref[r], length_of)
    live = slot < length_of

    def attend(step, carry):
        k = lax.rem(me // per_kv + 1 + step, KVH)
        key_at = pl.multiple_of(k * HD, HD)
        value_at = pl.multiple_of((KVH + k) * HD, HD)
        queries = jnp.concatenate(
            [gathered[k * per_kv + j, :head_rows, :] for j in range(per_kv)], axis=0
        )
        keys = kv_v[:, :, pl.ds(key_at, HD)].reshape(requests * window, HD)
        values = kv_v[:, :, pl.ds(value_at, HD)].reshape(requests * window, HD)
        scores = lax.dot_general(
            queries, keys, (((1,), (1,)), ((), ())), preferred_element_type=jnp.float32
        )
        cached = scores[:, :window]
        for r in range(1, requests):
            cached = jnp.where(
                request_of == r, scores[:, r * window : (r + 1) * window], cached
            )
        cached = jnp.where(live, cached * inv_root, LIVE_MIN)
        top = jnp.max(cached, axis=-1, keepdims=True)
        weights = jnp.where(live, jnp.exp(cached - top), 0.0)
        weights = weights.astype(jnp.bfloat16).astype(jnp.float32)
        weight_total = jnp.sum(weights, axis=-1, keepdims=True)
        spread = jnp.concatenate(
            [jnp.where(request_of == r, weights, 0.0) for r in range(requests)], axis=1
        ).astype(jnp.bfloat16)
        weighted = jnp.dot(spread, values, preferred_element_type=jnp.float32)
        blocks = []
        for j in range(per_kv):
            first = j * head_rows
            stats = jnp.zeros((rows, HD), jnp.float32)
            for u in range(heads):
                at = first + u * rows
                stats = jnp.where(lane == u, top[at : at + rows], stats)
                stats = jnp.where(lane == HD // 2 + u, weight_total[at : at + rows], stats)
            blocks.append(
                jnp.concatenate([weighted[first : first + head_rows], stats], axis=0)
            )
        for j in range(0, per_kv, 2):
            i = lax.rem((k * per_kv + j) // 2 - chip + chips, chips)
            o_own[i] = jnp.where(core == 0, blocks[j], blocks[j + 1])
            o_other[i] = jnp.where(core == 0, blocks[j + 1], blocks[j])
            to_mate(MERGE, i, o_other.at[i], o_mate.at[i]).start()
        return carry

    def merged(i):
        to_mate(MERGE, i, o_other.at[i], o_mate.at[i]).wait_recv()
        one = o_own[i, head_rows:, :]
        two = o_mate[i, head_rows:, :]
        top = jnp.maximum(one, two)
        scale_one = jnp.exp(one - top)
        scale_two = jnp.exp(two - top)
        weight_total = scale_one * pltpu.roll(one, HD // 2, 1) + scale_two * pltpu.roll(
            two, HD // 2, 1
        )
        parts = []
        for u in range(heads):
            at = u * rows
            parts.append(
                scale_one[:, u : u + 1] * o_own[i, at : at + rows, :]
                + scale_two[:, u : u + 1] * o_mate[i, at : at + rows, :]
            )
        parts.append(jnp.where(lane < HD // 2, top, pltpu.roll(weight_total, HD // 2, 1)))
        return jnp.concatenate(parts, axis=0)

    def merge_send(i):
        o_own[i] = merged(i)
        across(MERGE, i, o_own.at[i], o_recv.at[chip]).start()

    if chips == KVH:
        staggered(lambda i: attend(lax.rem(i - 1 + KVH, KVH), 0), merge_send)
    else:
        lax.fori_loop(0, KVH, attend, 0)
        each_peer(merge_send)
    o_recv[chip] = merged(0)

    my_kv = me // per_kv

    def unit_rows(u):
        return gathered[u * per_unit, head_rows : head_rows + 16, :].astype(jnp.float32)[:rows]

    new_keys = unit_rows(my_kv)
    new_values = unit_rows(KVH + my_kv)
    earlier_keys = pltpu.roll(new_keys, requests, 0)
    earlier_values = pltpu.roll(new_values, requests, 0)
    my_queries = gathered[me, :head_rows, :].astype(jnp.float32)
    second = lax.broadcasted_iota(jnp.int32, (rows, HD), 0) >= requests
    same = jnp.zeros((rows, HD), jnp.float32)
    earlier = jnp.zeros((rows, HD), jnp.float32)
    for u in range(heads):
        q = my_queries[u * rows : (u + 1) * rows]
        same = jnp.where(lane == u, jnp.sum(q * new_keys, axis=-1, keepdims=True), same)
        earlier = jnp.where(
            lane == u, jnp.sum(q * earlier_keys, axis=-1, keepdims=True), earlier
        )
    same = same * inv_root
    earlier = jnp.where(second, earlier * inv_root, LIVE_MIN)

    each_peer(lambda i: across(MERGE, i, o_own.at[i], o_recv.at[source_at(i)]).wait_recv())
    stats = [o_recv[d, head_rows:, :] for d in range(chips)]
    top = jnp.maximum(same, earlier)
    for d in range(chips):
        top = jnp.maximum(top, stats[d])
    same_weight = jnp.exp(same - top).astype(jnp.bfloat16).astype(jnp.float32)
    earlier_weight = jnp.exp(earlier - top).astype(jnp.bfloat16).astype(jnp.float32)
    denominator = same_weight + earlier_weight
    numerators = [
        same_weight[:, u : u + 1] * new_values + earlier_weight[:, u : u + 1] * earlier_values
        for u in range(heads)
    ]
    for d in range(chips):
        rescale = jnp.exp(stats[d] - top)
        denominator += rescale * pltpu.roll(stats[d], HD // 2, 1)
        for u in range(heads):
            numerators[u] += rescale[:, u : u + 1] * o_recv[d, u * rows : (u + 1) * rows, :]
    attended = jnp.concatenate(
        [numerators[u] / denominator[:, u : u + 1] for u in range(heads)], axis=1
    ).astype(jnp.bfloat16)

    half = width // 2

    def output(i):
        wo_copy(i).wait()
        y = jnp.dot(attended, wo_v[i], preferred_element_type=jnp.float32)
        first = jnp.concatenate([y[:, :half], y[:, half:width]], axis=0)
        second = jnp.concatenate([y[:, width : width + half], y[:, width + half :]], axis=0)
        p_other[i] = jnp.where(core == 0, second, first).astype(jnp.bfloat16)
        p_own[i] = jnp.where(core == 0, first, second).astype(jnp.bfloat16)
        to_mate(PROJ, i, p_other.at[i], p_mate.at[i]).start()

    def paired(i):
        to_mate(PROJ, i, p_other.at[i], p_mate.at[i]).wait_recv()
        return p_own[i].astype(jnp.float32) + p_mate[i].astype(jnp.float32)

    def output_send(i):
        p_own[i] = paired(i).astype(jnp.bfloat16)
        across(PROJ, i, p_own.at[i], p_recv.at[chip]).start()

    staggered(output, output_send)
    summed = paired(0)
    p_recv[chip] = jnp.zeros(p_recv.shape[1:], jnp.bfloat16)
    each_peer(lambda i: across(PROJ, i, p_own.at[i], p_recv.at[source_at(i)]).wait_recv())
    summed = summed + jnp.sum(p_recv[...].astype(jnp.float32), axis=0)
    summed = jnp.concatenate([summed[:rows], summed[rows:]], axis=1)
    for s in range(steps):
        out_ref[s] = summed[s * requests : (s + 1) * requests]

    to_mate(SQ, 0, sq_pair.at[core], sq_pair.at[core]).wait_send()

    def drain(i):
        across(SQ, i, sq_buf.at[chip], sq_buf.at[chip]).wait_send()
        across(QKV, i, q_own.at[i], q_recv.at[chip]).wait_send()
        across(GATHER, i, gathered.at[me], gathered.at[me]).wait_send()
        across(MERGE, i, o_own.at[i], o_recv.at[chip]).wait_send()
        across(PROJ, i, p_own.at[i], p_recv.at[chip]).wait_send()

    def drain_mate(i):
        to_mate(QKV, i, q_other.at[i], q_mate.at[i]).wait_send()
        to_mate(GATHER, i, gathered.at[me], gathered.at[me]).wait_send()
        to_mate(MERGE, i, o_other.at[i], o_mate.at[i]).wait_send()
        to_mate(PROJ, i, p_other.at[i], p_mate.at[i]).wait_send()

    each_peer(drain)
    each_chip(drain_mate)


def on_device(n, residual, norm_gain, w_query, w_keyval, w_out, kv_cache, lengths):
    steps, requests, width = residual.shape
    rows = steps * requests
    heads = QH // n
    columns = heads * HD
    chips = n // 2
    halfway = HD // 2
    frequency = 500000.0 ** (-2.0 * jnp.arange(halfway, dtype=jnp.float32) / HD)
    frequency = jnp.concatenate([frequency, frequency]).reshape(1, HD)

    gather_rows = ((heads + 1) * rows + 15) // 16 * 16
    vmem = pl.BlockSpec(memory_space=pltpu.VMEM)
    anywhere = pl.BlockSpec(memory_space=pl.ANY)
    bf16 = jnp.bfloat16
    f32 = jnp.float32
    summed = pl.pallas_call(
        functools.partial(kernel, n),
        out_shape=jax.ShapeDtypeStruct((steps, requests, width), f32),
        in_specs=[pl.BlockSpec(memory_space=pltpu.SMEM), vmem, vmem, vmem]
        + [anywhere] * 4,
        out_specs=vmem,
        scratch_shapes=[
            pltpu.VMEM((chips, width, 2 * columns), bf16),
            pltpu.VMEM(w_keyval.shape, bf16),
            pltpu.VMEM((chips, w_out.shape[0], 2 * width), bf16),
            pltpu.VMEM(kv_cache.shape, bf16),
            pltpu.VMEM((2, 1, HD), f32),
            pltpu.VMEM((chips, 1, HD), f32),
            pltpu.VMEM((rows, w_keyval.shape[1]), f32),
        ]
        + [pltpu.VMEM((chips, rows, columns + HD), f32)] * 4
        + [pltpu.VMEM((n, gather_rows, HD), bf16)]
        + [pltpu.VMEM((chips, (heads + 1) * rows, HD), f32)] * 4
        + [pltpu.VMEM((chips, 2 * rows, width // 2), bf16)] * 4
        + [
            pltpu.SemaphoreType.DMA((chips,)),
            pltpu.SemaphoreType.DMA,
            pltpu.SemaphoreType.DMA((chips,)),
            pltpu.SemaphoreType.DMA,
            pltpu.SemaphoreType.DMA((5, n)),
            pltpu.SemaphoreType.DMA((5, n)),
        ],
        compiler_params=pltpu.CompilerParams(
            collective_id=0, has_side_effects=True, vmem_limit_bytes=56 * 2**20
        ),
    )(lengths, residual, norm_gain, frequency, w_query, w_keyval, w_out, kv_cache)
    return (residual.astype(f32) + summed).astype(bf16)


def solution(mesh):
    placed = (
        P(None, "groups", "tp"),
        P("tp"),
        P("tp", None),
        P("tp", None),
        P("tp", None),
        P("groups", "tp", None),
        P("groups"),
    )
    return jax.shard_map(
        functools.partial(on_device, mesh.shape["tp"]),
        mesh=mesh,
        in_specs=placed,
        out_specs=P(None, "groups", "tp"),
        check_vma=False,
    )
```
